32 devices in a mesh: group: 2 (over x), src: 4 (over z), tile: 4 (over y, core).
Axes of the slice: x: 2, y: 2, z: 4, core: 2. Of those that a mesh axis runs over, the one named last changes fastest.
Arguments:
- mask_param: float32 [2048, 256], P(('group', 'tile')), parts along dimension 0, may hold values from -6 to 6
- target_image: float32 [2048, 256], P(('group', 'tile')), parts along dimension 0, may hold values from 0 to 1
- source_weights: float32 [128], P(('group', 'src')), parts along dimension 0, may hold values from 0.36 to 8.2
- source_shifts: int32 [64, 2], P('src'), may hold values from -16 to 16, as said below
- pupil_map: float32 [2, 32, 32], replicated, may hold values from -1.4 to 1.4, as said below
Outputs:
- mask_final: float32 [2048, 256], P(('group', 'tile')), parts along dimension 0
- weights_final: float32 [128], P(('group', 'src')), parts along dimension 0
The draws below stay inside these ranges and needn't reach their ends.
There are 2 independent parts, one for each index of `group`. The reference program is written for one: setup_inputs(seed, part) draws one part's arguments, and reference() takes and returns one part's arrays. A program takes and returns all parts, laid end to end along the dimension named above; an argument that names none is the same for every part. Nothing has to cross between parts.
Inputs may be any that keep to these rules, and one draw needn't show every extreme that they name: `source_shifts`: each of the two columns takes the value 16 on some source and the value -16 on another. `pupil_map`: zero outside the disc of radius 32 // 2 - 1 around box index (16, 16).
All inputs are finite; a program needn't handle non-finite values.
Results may differ from the reference program's by a relative error of at most 0.0003.
Values sent between devices are 32-bit elements; how exact they have to be, the bound alone decides.
A program may use at most 64 MiB of HBM per device.

```python
import math
import jax
import jax.numpy as jnp
from jax import lax

CLIP_TILE = 256
MARGIN = 64
PUPIL_BOX = 32
MAX_SHIFT = 16
OUTER_STEPS = 1
INNER_STEPS = 2
SOURCES = 64
TILES_ALL = 4
CLIP_ROWS = 1024
WINDOW = 384


def draw_target_image(key, part):
    level = jax.random.uniform(key, (CLIP_ROWS, CLIP_TILE), jnp.float32)
    ramp = 0.3 + 0.7 * (jnp.arange(CLIP_ROWS, dtype=jnp.float32) / CLIP_ROWS)[:, None]
    return level * ramp


def draw_source_weights(key, part):
    raw = jax.random.uniform(key, (SOURCES,), jnp.float32, -1.0, 1.0)
    ramp = 1.0 + 2.0 * jnp.arange(SOURCES, dtype=jnp.float32) / (SOURCES - 1)
    return jnp.exp(raw) * ramp


def draw_source_shifts(key, part):
    key_one, key_two = jax.random.split(key)
    values = jax.random.randint(key_one, (SOURCES, 2), -MAX_SHIFT, MAX_SHIFT + 1, dtype=jnp.int32)
    chosen = jax.random.permutation(key_two, SOURCES)[:4]
    ends = jnp.array([[1, 0], [-1, 0], [0, 1], [0, -1]], dtype=jnp.int32) * MAX_SHIFT
    return values.at[chosen].set(ends)


def draw_pupil_map(key, part):
    key_amp, key_phase = jax.random.split(key)
    offsets = jnp.arange(PUPIL_BOX, dtype=jnp.int32) - PUPIL_BOX // 2
    radius = PUPIL_BOX // 2 - 1
    inside = (offsets[:, None] * offsets[:, None] + offsets[None, :] * offsets[None, :] <= radius * radius).astype(jnp.float32)
    amplitude = jax.random.uniform(key_amp, (PUPIL_BOX, PUPIL_BOX), jnp.float32, 0.6, 1.4)
    phases = jax.random.uniform(key_phase, (PUPIL_BOX, PUPIL_BOX), jnp.float32, -1.0, 1.0)
    return jnp.stack([amplitude * jnp.cos(phases), amplitude * jnp.sin(phases)]) * inside[None]


def steps_of(rng, extent, cuts, low, top_value):
    level, own = 1.0, jax.random.fold_in(rng, 6)
    for axis_at, shards_of in cuts:
        heights = jnp.exp(jax.random.uniform(jax.random.fold_in(own, axis_at), (shards_of,), jnp.float32, low / len(cuts), top_value / len(cuts)))
        level = level * jnp.repeat(heights, extent[axis_at] // shards_of).reshape([-1 if axis == axis_at else 1 for axis in range(len(extent))])
    return level


def noise(rng, shape, width, most, cuts=(), kind=jnp.bfloat16):
    gain = steps_of(rng, shape, cuts, -0.22, 0.18) if cuts else 1.0
    entries = jax.random.normal(rng, shape, jnp.float32) * width * gain
    return jnp.minimum(jnp.maximum(entries, -most), most).astype(kind)


def setup_inputs(seed: int = 0, part: int = 0) -> dict:
    key_of = jax.random.split(jax.random.key(seed), 6)
    own_keys = jax.random.split(jax.random.fold_in(key_of[5], part), 6)
    mask_param = noise(own_keys[0], (CLIP_ROWS, CLIP_TILE), 1.0, 6.0, ((0, 4),), jnp.float32)
    target_image = draw_target_image(jax.random.fold_in(jax.random.fold_in(key_of[5], part), 71), part)
    source_weights = draw_source_weights(jax.random.fold_in(jax.random.fold_in(key_of[5], part), 71), part)
    source_shifts = draw_source_shifts(jax.random.fold_in(key_of[5], 71), part)
    pupil_map = draw_pupil_map(jax.random.fold_in(key_of[5], 71), part)
    return dict(mask_param=mask_param, target_image=target_image, source_weights=source_weights, source_shifts=source_shifts, pupil_map=pupil_map)


highest = lax.Precision.HIGHEST
mask_rate = 0.5
weight_rate = 0.3
tiny_eps = 1e-06

def matmul(left, right):
    return jnp.dot(left, right, precision=highest)

def einsum_hi(formula, left, right):
    return jnp.einsum(formula, left, right, precision=highest)

def phase_table(freq_list, pixels, period):
    product = jnp.mod(freq_list[:, None] * pixels[None, :], period)
    angles = product.astype(jnp.float32) * (2.0 * math.pi / period)
    return (jnp.cos(angles), jnp.sin(angles))

def make_tables(period, tile_len, margin, box_len, max_shift):
    wide_freqs = jnp.arange(box_len + 2 * max_shift, dtype=jnp.int32) - (box_len // 2 + max_shift)
    box_freqs = jnp.arange(box_len, dtype=jnp.int32) - box_len // 2
    pixels = jnp.arange(tile_len, dtype=jnp.int32)
    rows_fwd = phase_table(wide_freqs, jnp.arange(period, dtype=jnp.int32), period)
    cols_fwd = phase_table(wide_freqs, pixels, period)
    rows_inv = phase_table(box_freqs, pixels + margin, period)
    cols_inv = phase_table(box_freqs, pixels, period)
    return (rows_fwd, cols_fwd, rows_inv, cols_inv)

def selectors(shifts, box_len, max_shift):
    freq_width = box_len + 2 * max_shift
    columns = jnp.arange(freq_width, dtype=jnp.int32)[None, None, :]
    box_base = jnp.arange(box_len, dtype=jnp.int32)[None, :] + max_shift
    rows_at = box_base + shifts[:, 0:1]
    cols_at = box_base + shifts[:, 1:2]
    sel_rows = (rows_at[:, :, None] == columns).astype(jnp.float32)
    sel_cols = (cols_at[:, :, None] == columns).astype(jnp.float32)
    return (sel_rows, sel_cols)

def spectrum(window_mask, rows_fwd, cols_fwd, norm_scale):
    first_re = matmul(rows_fwd[0], window_mask)
    first_im = -matmul(rows_fwd[1], window_mask)
    spec_re = matmul(first_re, cols_fwd[0].T) + matmul(first_im, cols_fwd[1].T)
    spec_im = matmul(first_im, cols_fwd[0].T) - matmul(first_re, cols_fwd[1].T)
    return jnp.stack([spec_re, spec_im]) * norm_scale

def make_fields(spec, sel_rows, sel_cols, pupil_map, rows_inv, cols_inv):
    picked = einsum_hi('sij,cjl->csil', sel_rows, spec)
    picked = einsum_hi('csil,sml->csim', picked, sel_cols)
    lit_re = pupil_map[0] * picked[0] - pupil_map[1] * picked[1]
    lit_im = pupil_map[0] * picked[1] + pupil_map[1] * picked[0]
    mid_re = einsum_hi('kx,skl->sxl', rows_inv[0], lit_re) - einsum_hi('kx,skl->sxl', rows_inv[1], lit_im)
    mid_im = einsum_hi('kx,skl->sxl', rows_inv[0], lit_im) + einsum_hi('kx,skl->sxl', rows_inv[1], lit_re)
    field_re = einsum_hi('sxl,ly->sxy', mid_re, cols_inv[0]) - einsum_hi('sxl,ly->sxy', mid_im, cols_inv[1])
    field_im = einsum_hi('sxl,ly->sxy', mid_re, cols_inv[1]) + einsum_hi('sxl,ly->sxy', mid_im, cols_inv[0])
    return (field_re, field_im)

def spectral_grad(field_re, field_im, misfit, factor, sel_rows, sel_cols, pupil_map, rows_inv, cols_inv):
    hit_re = misfit[None] * field_re
    hit_im = misfit[None] * field_im
    half_re = einsum_hi('sxy,ly->sxl', hit_re, cols_inv[0]) + einsum_hi('sxy,ly->sxl', hit_im, cols_inv[1])
    half_im = einsum_hi('sxy,ly->sxl', hit_im, cols_inv[0]) - einsum_hi('sxy,ly->sxl', hit_re, cols_inv[1])
    box_re = einsum_hi('kx,sxl->skl', rows_inv[0], half_re) + einsum_hi('kx,sxl->skl', rows_inv[1], half_im)
    box_im = einsum_hi('kx,sxl->skl', rows_inv[0], half_im) - einsum_hi('kx,sxl->skl', rows_inv[1], half_re)
    weight_col = factor[:, None, None]
    back_re = (pupil_map[0] * box_re + pupil_map[1] * box_im) * weight_col
    back_im = (pupil_map[0] * box_im - pupil_map[1] * box_re) * weight_col
    stacked = jnp.stack([back_re, back_im])
    placed = einsum_hi('csim,sij->csjm', stacked, sel_rows)
    return einsum_hi('csjm,sml->cjl', placed, sel_cols)

def adjoint(grad_spec, rows_fwd, cols_fwd, norm_scale):
    vals_re = matmul(grad_spec[0], cols_fwd[0]) - matmul(grad_spec[1], cols_fwd[1])
    vals_im = matmul(grad_spec[0], cols_fwd[1]) + matmul(grad_spec[1], cols_fwd[0])
    return (matmul(rows_fwd[0].T, vals_re) - matmul(rows_fwd[1].T, vals_im)) * norm_scale

def assemble(windows, margin, tile_len):
    core = windows[:, margin:margin + tile_len]
    top_rim = windows[:, :margin]
    low_rim = windows[:, margin + tile_len:]
    empty = jnp.zeros_like(top_rim[:1])
    from_next = jnp.concatenate([top_rim[1:], empty], axis=0)
    from_prev = jnp.concatenate([empty, low_rim[:-1]], axis=0)
    core = core.at[:, tile_len - margin:].add(from_next)
    core = core.at[:, :margin].add(from_prev)
    return core.reshape(-1, tile_len)

def reference(mask_param, target_image, source_weights, source_shifts, pupil_map):
    tables = make_tables(WINDOW, CLIP_TILE, MARGIN, PUPIL_BOX, MAX_SHIFT)
    rows_fwd, cols_fwd, rows_inv, cols_inv = tables
    sel_rows, sel_cols = selectors(source_shifts, PUPIL_BOX, MAX_SHIFT)
    norm_scale = 1.0 / (WINDOW * CLIP_TILE)
    pixel_count = CLIP_ROWS * CLIP_TILE
    target_tiles = target_image.reshape(TILES_ALL, CLIP_TILE, CLIP_TILE)
    tile_ids = jnp.arange(TILES_ALL, dtype=jnp.int32)
    params = mask_param
    weights = source_weights

    def tile_image(padded, tile_id, weights, dose_total):
        window_mask = lax.dynamic_slice_in_dim(padded, tile_id * CLIP_TILE, WINDOW, 0)
        spec = spectrum(window_mask, rows_fwd, cols_fwd, norm_scale)
        field_re, field_im = make_fields(spec, sel_rows, sel_cols, pupil_map, rows_inv, cols_inv)
        powers = field_re * field_re + field_im * field_im
        intensity = einsum_hi('s,sxy->xy', weights, powers) / dose_total
        misfit = intensity - lax.dynamic_index_in_dim(target_tiles, tile_id, 0, keepdims=False)
        return (field_re, field_im, powers, intensity, misfit)
    for outer_step in range(OUTER_STEPS):
        for inner_step in range(INNER_STEPS):
            mask_field = jax.nn.sigmoid(params)
            padded = jnp.pad(mask_field, ((MARGIN, MARGIN), (0, 0)))
            dose_total = jnp.sum(weights)
            factor = 2.0 * weights / dose_total

            def window_grad(tile_id):
                field_re, field_im, powers, intensity, misfit = tile_image(padded, tile_id, weights, dose_total)
                grad_spec = spectral_grad(field_re, field_im, misfit, factor, sel_rows, sel_cols, pupil_map, rows_inv, cols_inv)
                return adjoint(grad_spec, rows_fwd, cols_fwd, norm_scale)
            windows = lax.map(window_grad, tile_ids)
            mask_grad = assemble(windows, MARGIN, CLIP_TILE) * (mask_field * (1.0 - mask_field))
            rms = jnp.sqrt(jnp.sum(mask_grad * mask_grad) / pixel_count + tiny_eps)
            params = params - mask_rate * mask_grad / rms
        mask_field = jax.nn.sigmoid(params)
        padded = jnp.pad(mask_field, ((MARGIN, MARGIN), (0, 0)))
        dose_total = jnp.sum(weights)

        def source_part(tile_id):
            field_re, field_im, powers, intensity, misfit = tile_image(padded, tile_id, weights, dose_total)
            return (einsum_hi('xy,sxy->s', misfit, powers) - jnp.sum(misfit * intensity)) / dose_total
        source_grad = lax.optimization_barrier(jnp.sum(lax.map(source_part, tile_ids), axis=0))
        spread = jnp.sqrt(jnp.sum(source_grad * source_grad) / SOURCES + tiny_eps)
        weights = weights * jnp.exp(-weight_rate * source_grad / spread)
    return (params, weights)
```

```python
import functools
import math

import jax
import jax.numpy as jnp
import numpy as np
from jax import lax
from jax.experimental import pallas as pl
from jax.experimental.pallas import tpu as pltpu
from jax.sharding import PartitionSpec as P

MARGIN = 64
MAX_SHIFT = 16
INNER_STEPS = 2
MESH = pl.DeviceIdType.MESH
mask_rate = 0.5
weight_rate = 0.3
tiny_eps = 1e-06
f32 = jnp.float32
bf16 = jnp.bfloat16


def angle(freqs, pixels, period):
    return np.mod(np.outer(freqs, pixels), period) * (2.0 * math.pi / period)


def dirichlet(pixels, period, box):
    grid = 2 * box
    diffs = np.arange(-(box - 1), box)
    left = angle(pixels, diffs, period)
    right = angle(diffs, np.arange(grid), grid)
    return (np.cos(left) @ np.cos(right) + np.sin(left) @ np.sin(right)) / grid


def tables(period, tile, box):
    grid = 2 * box
    wide = np.arange(grid) - box
    row = angle(wide, np.arange(period), period)
    col = angle(wide, np.arange(tile), period)
    g = angle(np.arange(grid), np.arange(grid), grid)
    c, s = np.cos(g), np.sin(g)
    k1 = dirichlet(np.arange(tile) + MARGIN, period, box)
    k2 = dirichlet(np.arange(tile), period, box)
    k2d = np.concatenate([k2.T, k2.T], 0)
    return dict(
        rf=np.concatenate([np.cos(row), np.sin(row)], 0),
        cf=np.concatenate([np.cos(col), np.sin(col)], 0).T,
        c2=np.block([[c, s], [-s, c]]),
        c2t=np.block([[c, -s], [s, c]]),
        cs=np.concatenate([c, s], 0),
        k1=k1,
        k1t=k1.T,
        k2d=k2d,
        k2dt=k2d.T,
        col=np.block([[np.cos(col), np.sin(col)], [-np.sin(col), np.cos(col)]]),
        rfa=np.concatenate([np.cos(row), -np.sin(row)], 0).T,
    )


NAMES = ("rf", "cf", "c2", "c2t", "cs", "k1", "k1t", "k2d", "k2dt", "col", "rfa")


def split_np(value):
    value = value.astype(np.float32)
    high = value.astype(jnp.bfloat16)
    low = (value - high.astype(np.float32)).astype(jnp.bfloat16)
    return high, low


def split(value):
    high = value.astype(bf16)
    return high, (value - high.astype(f32)).astype(bf16)


def dot(a, b):
    return jnp.dot(a, b, preferred_element_type=f32)


def dot3(a, b):
    return dot(a[0], b[0]) + (dot(a[0], b[1]) + dot(a[1], b[0]))


def kernel(ns, nt, scale, *refs):
    mask_ref, target_ref, wl_ref, wb_ref, pa_ref, pb_ref = refs[:6]
    consts = {
        name: (refs[6 + 2 * i], refs[7 + 2 * i]) for i, name in enumerate(NAMES)
    }
    refs = refs[6 + 2 * len(NAMES):]
    mask_out, weights_out = refs[:2]
    (params, grid, halo, dose_buf, power_buf, back_buf, next_buf, sq_buf, sg_buf, ss_buf,
     src_send, src_recv, tile_send, tile_recv) = refs[2:]
    group = lax.axis_index("group")
    src = lax.axis_index("src")
    tile = lax.axis_index("tile")
    size = mask_ref.shape[1]
    period = size + 2 * MARGIN
    count = wb_ref.shape[0]
    width = pa_ref.shape[1]
    half = width // 2

    def table(name):
        return consts[name][0][...], consts[name][1][...]

    def src_peer(r):
        return (group, lax.rem(src + r, ns), tile)

    def tile_peer(r):
        return (group, src, lax.rem(tile + r, nt))

    pending = []
    used = dict(src=0, tile=0)

    def start(axis, source, target, peer):
        at = used[axis]
        used[axis] = at + 1
        sends, recvs = (src_send, src_recv) if axis == "src" else (tile_send, tile_recv)
        copy = pltpu.make_async_remote_copy(
            src_ref=source, dst_ref=target, send_sem=sends.at[at], recv_sem=recvs.at[at],
            device_id=peer, device_id_type=MESH,
        )
        copy.start()
        pending.append(copy)
        return copy

    def spread_src(buf):
        return [start("src", buf.at[src], buf.at[src], src_peer(r)) for r in range(1, ns)]

    def spread_tile(buf):
        return [start("tile", buf.at[tile], buf.at[tile], tile_peer(r)) for r in range(1, nt)]

    def landed(copies):
        for copy in copies:
            copy.wait_recv()

    def total(buf, peers):
        value = buf[0]
        for i in range(1, peers):
            value = value + buf[i]
        return value

    barrier = pltpu.get_barrier_semaphore()
    for r in range(1, ns):
        pl.semaphore_signal(barrier, inc=1, device_id=src_peer(r), device_id_type=MESH)
    for r in range(1, nt):
        pl.semaphore_signal(barrier, inc=1, device_id=tile_peer(r), device_id_type=MESH)
    pl.semaphore_wait(barrier, ns + nt - 2)

    up = start("tile", mask_ref.at[pl.ds(size - MARGIN, MARGIN)], halo.at[0], tile_peer(1))
    down = start("tile", mask_ref.at[pl.ds(0, MARGIN)], halo.at[1], tile_peer(nt - 1))
    dose_buf[src] = wl_ref[...]
    dose_copies = spread_src(dose_buf)
    params[pl.ds(MARGIN, size)] = mask_ref[...]
    landed([up, down])
    params[pl.ds(0, MARGIN)] = halo[0]
    params[pl.ds(MARGIN + size, MARGIN)] = halo[1]
    landed(dose_copies)
    dose = jnp.sum(total(dose_buf, ns)[0:1], axis=1, keepdims=True)
    inv_dose = 1.0 / dose

    has_prev = (tile > 0).astype(f32)
    has_next = (tile < nt - 1).astype(f32)
    row_id = lax.broadcasted_iota(jnp.int32, (period, size), 0)
    keep = jnp.where(row_id < MARGIN, has_prev, jnp.where(row_id >= MARGIN + size, has_next, 1.0))
    lane = lax.broadcasted_iota(jnp.int32, (half, width), 1)
    sign = jnp.where(lane < half, 1.0, -1.0).astype(f32)

    def swap(value):
        return pltpu.roll(value, half, 1)

    def sigmoid_mask():
        return keep / (1.0 + jnp.exp(-params[...]))

    def imaging(mask, step):
        first = dot3(table("rf"), split(mask))
        quad = dot3(split(first), table("cf")) * scale
        spec = sign * quad[:half] - swap(quad[half:])
        spec_swap = swap(spec)
        parts = []
        for s in range(count):
            rows = pl.ds(s * half, half)
            parts.append(pa_ref[rows] * spec + pb_ref[rows] * spec_swap)
        lit = jnp.concatenate(parts, 0)
        mid = dot3(split(lit), table("c2"))
        cs = table("cs")
        power = jnp.zeros((half, width), f32)
        for s in range(count):
            both = dot3(cs, split(mid[s * half:(s + 1) * half]))
            z = both[:half] - sign * swap(both[half:])
            grid[s] = z
            power = power + wb_ref[s:s + 1] * (z * z)
        buf = power_buf.at[step]
        buf[src] = power
        landed(spread_src(buf))
        power = total(buf, ns)
        bright = dot3(split(dot3(table("k1"), split(power))), table("k2d")) * inv_dose
        misfit = bright - target_ref[...]
        pull = dot3(split(dot3(table("k1t"), split(misfit))), table("k2dt"))
        return bright, misfit, pull

    for step in range(INNER_STEPS):
        mask = sigmoid_mask()
        bright, misfit, pull = imaging(mask, step)
        cs = table("cs")
        parts = []
        for s in range(count):
            both = dot3(cs, split(pull * grid[s]))
            parts.append(both[:half] + sign * swap(both[half:]))
        box = dot3(split(jnp.concatenate(parts, 0)), table("c2t"))
        one = jnp.zeros((half, width), f32)
        two = jnp.zeros((half, width), f32)
        for s in range(count):
            rows = pl.ds(s * half, half)
            value = wb_ref[s:s + 1] * box[s * half:(s + 1) * half]
            one = one + pa_ref[rows] * value
            two = two + pb_ref[rows] * value
        buf = back_buf.at[step]
        buf[src] = (one + swap(two)) * (2.0 * scale * inv_dose)
        landed(spread_src(buf))
        own = next_buf.at[step]
        back = total(buf, ns)
        own[2] = back
        to_next = start("tile", own.at[2], own.at[0], tile_peer(1))
        to_prev = start("tile", own.at[2], own.at[1], tile_peer(nt - 1))
        col = table("col")

        def values(spectrum):
            wide = dot3(split(spectrum), col)
            return split(jnp.concatenate([wide[:, :size], wide[:, size:]], 0))

        grad = dot3(table("rfa"), values(back))
        landed([to_next, to_prev])
        rim = 2 * MARGIN
        high, low = consts["rfa"]
        tail = pl.ds(period - rim, rim)
        before = dot3((high[tail], low[tail]), values(own[0] * has_prev))
        after = dot3((high[0:rim], low[0:rim]), values(own[1] * has_next))
        grad = jnp.concatenate(
            [grad[:rim] + before, grad[rim:period - rim], grad[period - rim:] + after], 0
        )
        grad = grad * (mask * (1.0 - mask))
        core = grad[MARGIN:MARGIN + size]
        square = jnp.sum(core * core, axis=0, keepdims=True)
        square = jnp.sum(square, axis=1, keepdims=True)
        buf = sq_buf.at[step]
        buf[tile] = jnp.broadcast_to(square, sq_buf.shape[2:])
        landed(spread_tile(buf))
        square = total(buf, nt)[0:1, 0:1]
        rms = jnp.sqrt(square / float(nt * size * size) + tiny_eps)
        params[...] = params[...] - grad * (mask_rate / rms)
    mask_out[...] = params[pl.ds(MARGIN, size)]

    bright, misfit, pull = imaging(sigmoid_mask(), INNER_STEPS)
    level = jnp.sum(misfit * bright, axis=0, keepdims=True)
    level = jnp.sum(level, axis=1, keepdims=True)
    rows = []
    for s in range(count):
        rows.append(jnp.sum(pull * (grid[s] * grid[s]), axis=0, keepdims=True))
    sums = jnp.sum(jnp.concatenate(rows, 0), axis=1, keepdims=True)
    sums = (sums - level) * inv_dose
    lanes = lax.broadcasted_iota(jnp.int32, (count, 128), 1)
    ids = lax.broadcasted_iota(jnp.int32, (count, 128), 0)
    packed = jnp.sum(jnp.where(lanes == ids, sums, 0.0), axis=0, keepdims=True)
    sg_buf[tile] = jnp.broadcast_to(packed, (8, 128))
    landed(spread_tile(sg_buf))
    slope = total(sg_buf, nt)
    ss_buf[src] = slope * slope
    landed(spread_src(ss_buf))
    square = jnp.sum(total(ss_buf, ns)[0:1], axis=1, keepdims=True)
    spread = jnp.sqrt(square / float(count * ns) + tiny_eps)
    weights_out[...] = wl_ref[...] * jnp.exp(-weight_rate * slope / spread)
    for copy in pending:
        copy.wait_send()


def per_device(ns, nt, mask_param, target_image, source_weights, source_shifts, pupil_map):
    size = mask_param.shape[1]
    box = pupil_map.shape[1]
    half = 2 * box
    width = 2 * half
    count = source_weights.shape[0]
    period = size + 2 * MARGIN
    consts = []
    made = tables(period, size, box)
    for name in NAMES:
        high, low = split_np(made[name])
        consts += [jnp.asarray(high), jnp.asarray(low)]
    highest = lax.Precision.HIGHEST
    base = jnp.arange(box, dtype=jnp.int32)[None, :, None] + MAX_SHIFT
    columns = jnp.arange(half, dtype=jnp.int32)[None, None, :]
    sel_rows = (base + source_shifts[:, 0, None, None] == columns).astype(f32)
    sel_cols = (base + source_shifts[:, 1, None, None] == columns).astype(f32)
    moved = jnp.einsum("cim,sij->scjm", pupil_map, sel_rows, precision=highest)
    moved = jnp.einsum("scjm,sml->scjl", moved, sel_cols, precision=highest)
    re, im = moved[:, 0], moved[:, 1]
    pa = jnp.concatenate([re, re], -1).reshape(count * half, width)
    pb = jnp.concatenate([-im, im], -1).reshape(count * half, width)
    wl = jnp.broadcast_to(jnp.pad(source_weights, (0, 128 - count))[None], (8, 128))
    wb = jnp.broadcast_to(source_weights[:, None], (count, width))
    vmem = pl.BlockSpec(memory_space=pltpu.VMEM)
    src_sends = (ns - 1) * (2 + 2 * INNER_STEPS + 1)
    tile_sends = 2 + INNER_STEPS * (2 + nt - 1) + (nt - 1)
    args = (mask_param, target_image, wl, wb, pa, pb, *consts)
    mask_final, weights_final = pl.pallas_call(
        functools.partial(kernel, ns, nt, 1.0 / (period * size)),
        out_shape=(
            jax.ShapeDtypeStruct(mask_param.shape, f32),
            jax.ShapeDtypeStruct((8, 128), f32),
        ),
        in_specs=[vmem] * len(args),
        out_specs=(vmem, vmem),
        scratch_shapes=[
            pltpu.VMEM((period, size), f32),
            pltpu.VMEM((count, half, width), f32),
            pltpu.VMEM((2, MARGIN, size), f32),
            pltpu.VMEM((ns, 8, 128), f32),
            pltpu.VMEM((INNER_STEPS + 1, ns, half, width), f32),
            pltpu.VMEM((INNER_STEPS, ns, half, width), f32),
            pltpu.VMEM((INNER_STEPS, 3, half, width), f32),
            pltpu.VMEM((INNER_STEPS, nt, 8, 128), f32),
            pltpu.VMEM((nt, 8, 128), f32),
            pltpu.VMEM((ns, 8, 128), f32),
            pltpu.SemaphoreType.DMA((src_sends,)),
            pltpu.SemaphoreType.DMA((src_sends,)),
            pltpu.SemaphoreType.DMA((tile_sends,)),
            pltpu.SemaphoreType.DMA((tile_sends,)),
        ],
        compiler_params=pltpu.CompilerParams(
            collective_id=0, has_side_effects=True, vmem_limit_bytes=48 * 1024 * 1024
        ),
    )(*args)
    return mask_final, weights_final[0, :count]


def solution(mesh):
    in_specs = (
        P(("group", "tile"), None),
        P(("group", "tile"), None),
        P(("group", "src")),
        P("src", None),
        P(),
    )
    out_specs = (P(("group", "tile"), None), P(("group", "src")))
    return jax.shard_map(
        functools.partial(per_device, mesh.shape["src"], mesh.shape["tile"]),
        mesh=mesh, in_specs=in_specs, out_specs=out_specs, check_vma=False,
    )
```

```python
import functools
import math

import jax
import jax.numpy as jnp
import numpy as np
from jax import lax
from jax.experimental import pallas as pl
from jax.experimental.pallas import tpu as pltpu
from jax.sharding import PartitionSpec as P

MARGIN = 64
MAX_SHIFT = 16
INNER_STEPS = 2
MESH = pl.DeviceIdType.MESH
mask_rate = 0.5
weight_rate = 0.3
tiny_eps = 1e-06
f32 = jnp.float32
bf16 = jnp.bfloat16


def angle(freqs, pixels, period):
    return np.mod(np.outer(freqs, pixels), period) * (2.0 * math.pi / period)


def dirichlet(pixels, period, box):
    grid = 2 * box
    diffs = np.arange(-(box - 1), box)
    left = angle(pixels, diffs, period)
    right = angle(diffs, np.arange(grid), grid)
    return (np.cos(left) @ np.cos(right) + np.sin(left) @ np.sin(right)) / grid


def tables(period, tile, box):
    grid = 2 * box
    wide = np.arange(grid) - box
    row = angle(wide, np.arange(period), period)
    col = angle(wide, np.arange(tile), period)
    g = angle(np.arange(grid), np.arange(grid), grid)
    c, s = np.cos(g), np.sin(g)
    k1 = dirichlet(np.arange(tile) + MARGIN, period, box)
    k2 = dirichlet(np.arange(tile), period, box)
    k2d = np.concatenate([k2.T, np.zeros_like(k2.T)], 0)
    return dict(
        rf=np.concatenate([np.cos(row), np.sin(row)], 0),
        cf=np.concatenate([np.cos(col), np.sin(col)], 0).T,
        c2=np.block([[c, s], [-s, c]]),
        c2t=np.block([[c, -s], [s, c]]),
        cs=np.concatenate([c, s], 0),
        k1=k1,
        k1t=k1.T,
        k2d=k2d,
        k2dt=np.concatenate([k2, k2], 1),
        col=np.block([[np.cos(col), np.sin(col)], [-np.sin(col), np.cos(col)]]),
        rfa=np.concatenate([np.cos(row), -np.sin(row)], 0).T,
    )


LEFT = ("rf", "cs", "k1", "k1t", "rfa")
NAMES = ("rf", "cf", "c2", "c2t", "cs", "k1", "k1t", "k2d", "k2dt", "col", "rfa")


def split_np(value):
    value = value.astype(np.float32)
    high = value.astype(jnp.bfloat16)
    low = (value - high.astype(np.float32)).astype(jnp.bfloat16)
    return high, low


def packed(name, value):
    high, low = split_np(value)
    if name in ("c2", "c2t"):
        return np.block([[high, low], [high, np.zeros_like(low)]])
    if name in LEFT:
        return np.concatenate([high, high, low], 1)
    return np.concatenate([high, high, low], 0)


def split(value):
    high = value.astype(bf16)
    return high, (value - high.astype(f32)).astype(bf16)


def dot(a, b):
    return jnp.dot(a, b, preferred_element_type=f32)


def left_dot(table, value):
    high, low = split(value)
    return dot(table, jnp.concatenate([high, low, high], 0))


def right_dot(value, table):
    high, low = split(value)
    return dot(jnp.concatenate([high, low, high], 1), table)


def wide_dot(value, table):
    high, low = split(value)
    both = dot(jnp.concatenate([high, low], 1), table)
    width = value.shape[1]
    return both[:, :width] + both[:, width:]


def kernel(ns, nt, scale, *refs):
    mask_ref, target_ref, wl_ref, wb_ref, pa_ref, pb_ref = refs[:6]
    consts = {name: refs[6 + i] for i, name in enumerate(NAMES)}
    refs = refs[6 + len(NAMES):]
    mask_out, weights_out = refs[:2]
    (params, grid, halo, dose_buf, power_buf, back_buf, next_buf, sq_buf, sg_buf, ss_buf,
     src_send, src_recv, tile_send, tile_recv) = refs[2:]
    group = lax.axis_index("group")
    src = lax.axis_index("src")
    tile = lax.axis_index("tile")
    size = mask_ref.shape[1]
    period = size + 2 * MARGIN
    count = wb_ref.shape[0]
    width = pa_ref.shape[1]
    half = width // 2

    def table(name):
        return consts[name][...]

    def src_peer(r):
        return (group, lax.rem(src + r, ns), tile)

    def tile_peer(r):
        return (group, src, lax.rem(tile + r, nt))

    pending = []
    used = dict(src=0, tile=0)

    def start(axis, source, target, peer):
        at = used[axis]
        used[axis] = at + 1
        sends, recvs = (src_send, src_recv) if axis == "src" else (tile_send, tile_recv)
        copy = pltpu.make_async_remote_copy(
            src_ref=source, dst_ref=target, send_sem=sends.at[at], recv_sem=recvs.at[at],
            device_id=peer, device_id_type=MESH,
        )
        copy.start()
        pending.append(copy)
        return copy

    def spread_src(buf):
        return [start("src", buf.at[src], buf.at[src], src_peer(r)) for r in range(1, ns)]

    def spread_tile(buf):
        return [start("tile", buf.at[tile], buf.at[tile], tile_peer(r)) for r in range(1, nt)]

    def landed(copies):
        for copy in copies:
            copy.wait_recv()

    def total(buf, peers):
        value = buf[0]
        for i in range(1, peers):
            value = value + buf[i]
        return value

    barrier = pltpu.get_barrier_semaphore()
    for r in range(1, ns):
        pl.semaphore_signal(barrier, inc=1, device_id=src_peer(r), device_id_type=MESH)
    for r in range(1, nt):
        pl.semaphore_signal(barrier, inc=1, device_id=tile_peer(r), device_id_type=MESH)
    pl.semaphore_wait(barrier, ns + nt - 2)

    up = start("tile", mask_ref.at[pl.ds(size - MARGIN, MARGIN)], halo.at[0], tile_peer(1))
    down = start("tile", mask_ref.at[pl.ds(0, MARGIN)], halo.at[1], tile_peer(nt - 1))
    dose_buf[src] = wl_ref[...]
    dose_copies = spread_src(dose_buf)
    params[pl.ds(MARGIN, size)] = mask_ref[...]
    landed([up, down])
    params[pl.ds(0, MARGIN)] = halo[0]
    params[pl.ds(MARGIN + size, MARGIN)] = halo[1]
    landed(dose_copies)
    dose = jnp.sum(total(dose_buf, ns)[0:1], axis=1, keepdims=True)
    inv_dose = 1.0 / dose

    has_prev = (tile > 0).astype(f32)
    has_next = (tile < nt - 1).astype(f32)
    row_id = lax.broadcasted_iota(jnp.int32, (period, size), 0)
    keep = jnp.where(row_id < MARGIN, has_prev, jnp.where(row_id >= MARGIN + size, has_next, 1.0))
    lane = lax.broadcasted_iota(jnp.int32, (half, width), 1)
    sign = jnp.where(lane < half, 1.0, -1.0).astype(f32)

    def swap(value):
        return pltpu.roll(value, half, 1)

    def sigmoid_mask():
        return keep / (1.0 + jnp.exp(-params[...]))

    def imaging(mask, step):
        quad = right_dot(left_dot(table("rf"), mask), table("cf")) * scale
        spec = sign * quad[:half] - swap(quad[half:])
        spec_swap = swap(spec)
        parts = []
        for s in range(count):
            rows = pl.ds(s * half, half)
            parts.append(pa_ref[rows] * spec + pb_ref[rows] * spec_swap)
        lit = jnp.concatenate(parts, 0)
        mid = wide_dot(lit, table("c2"))
        cs = table("cs")
        power = jnp.zeros((half, width), f32)
        for s in range(0, count, 2):
            pair = [mid[i * half:(i + 1) * half] for i in range(s, s + 2)]
            both = left_dot(cs, jnp.concatenate(pair, 1))
            for i in range(2):
                one = both[:, i * width:(i + 1) * width]
                z = one[:half] - sign * swap(one[half:])
                grid[s + i] = z
                power = power + wb_ref[s + i:s + i + 1] * (z * z)
        power = power + swap(power)
        power = jnp.where(lane[:half // 2] < half, power[:half // 2], power[half // 2:])
        buf = power_buf.at[step]
        buf[src] = power
        landed(spread_src(buf))
        power = total(buf, ns)
        power = jnp.concatenate([power, swap(power)], 0)
        bright = right_dot(left_dot(table("k1"), power), table("k2d")) * inv_dose
        misfit = bright - target_ref[...]
        pull = right_dot(left_dot(table("k1t"), misfit), table("k2dt"))
        return bright, misfit, pull

    for step in range(INNER_STEPS):
        mask = sigmoid_mask()
        bright, misfit, pull = imaging(mask, step)
        cs = table("cs")
        parts = []
        for s in range(0, count, 2):
            pair = [pull * grid[i] for i in range(s, s + 2)]
            both = left_dot(cs, jnp.concatenate(pair, 1))
            for i in range(2):
                part = both[:, i * width:(i + 1) * width]
                parts.append(part[:half] + sign * swap(part[half:]))
        box = wide_dot(jnp.concatenate(parts, 0), table("c2t"))
        one = jnp.zeros((half, width), f32)
        two = jnp.zeros((half, width), f32)
        for s in range(count):
            rows = pl.ds(s * half, half)
            value = wb_ref[s:s + 1] * box[s * half:(s + 1) * half]
            one = one + pa_ref[rows] * value
            two = two + pb_ref[rows] * value
        buf = back_buf.at[step]
        buf[src] = (one + swap(two)) * (2.0 * scale * inv_dose)
        landed(spread_src(buf))
        own = next_buf.at[step]
        back = total(buf, ns)
        own[2] = back
        to_next = start("tile", own.at[2], own.at[0], tile_peer(1))
        to_prev = start("tile", own.at[2], own.at[1], tile_peer(nt - 1))
        col = table("col")

        def values(spectrum):
            wide = right_dot(spectrum, col)
            return jnp.concatenate([wide[:, :size], wide[:, size:]], 0)

        grad = left_dot(table("rfa"), values(back))
        landed([to_next, to_prev])
        rim = 2 * MARGIN
        rfa = consts["rfa"]
        before = left_dot(rfa[pl.ds(period - rim, rim)], values(own[0] * has_prev))
        after = left_dot(rfa[pl.ds(0, rim)], values(own[1] * has_next))
        grad = jnp.concatenate(
            [grad[:rim] + before, grad[rim:period - rim], grad[period - rim:] + after], 0
        )
        grad = grad * (mask * (1.0 - mask))
        core = grad[MARGIN:MARGIN + size]
        square = jnp.sum(core * core, axis=0, keepdims=True)
        square = jnp.sum(square, axis=1, keepdims=True)
        buf = sq_buf.at[step]
        buf[tile] = jnp.broadcast_to(square, sq_buf.shape[2:])
        landed(spread_tile(buf))
        square = total(buf, nt)[0:1, 0:1]
        rms = jnp.sqrt(square / float(nt * size * size) + tiny_eps)
        params[...] = params[...] - grad * (mask_rate / rms)
    mask_out[...] = params[pl.ds(MARGIN, size)]

    bright, misfit, pull = imaging(sigmoid_mask(), INNER_STEPS)
    level = jnp.sum(misfit * bright, axis=0, keepdims=True)
    level = jnp.sum(level, axis=1, keepdims=True)
    rows = []
    for s in range(count):
        rows.append(jnp.sum(pull * (grid[s] * grid[s]), axis=0, keepdims=True))
    sums = jnp.sum(jnp.concatenate(rows, 0), axis=1, keepdims=True)
    sums = (sums - level) * inv_dose
    lanes = lax.broadcasted_iota(jnp.int32, (count, 128), 1)
    ids = lax.broadcasted_iota(jnp.int32, (count, 128), 0)
    ordered = jnp.sum(jnp.where(lanes == ids, sums, 0.0), axis=0, keepdims=True)
    sg_buf[tile] = jnp.broadcast_to(ordered, (8, 128))
    landed(spread_tile(sg_buf))
    slope = total(sg_buf, nt)
    ss_buf[src] = slope * slope
    landed(spread_src(ss_buf))
    square = jnp.sum(total(ss_buf, ns)[0:1], axis=1, keepdims=True)
    spread = jnp.sqrt(square / float(count * ns) + tiny_eps)
    weights_out[...] = wl_ref[...] * jnp.exp(-weight_rate * slope / spread)
    for copy in pending:
        copy.wait_send()


def per_device(ns, nt, mask_param, target_image, source_weights, source_shifts, pupil_map):
    size = mask_param.shape[1]
    box = pupil_map.shape[1]
    half = 2 * box
    width = 2 * half
    count = source_weights.shape[0]
    period = size + 2 * MARGIN
    consts = []
    made = tables(period, size, box)
    for name in NAMES:
        consts.append(jnp.asarray(packed(name, made[name])))
    highest = lax.Precision.HIGHEST
    base = jnp.arange(box, dtype=jnp.int32)[None, :, None] + MAX_SHIFT
    columns = jnp.arange(half, dtype=jnp.int32)[None, None, :]
    sel_rows = (base + source_shifts[:, 0, None, None] == columns).astype(f32)
    sel_cols = (base + source_shifts[:, 1, None, None] == columns).astype(f32)
    moved = jnp.einsum("cim,sij->scjm", pupil_map, sel_rows, precision=highest)
    moved = jnp.einsum("scjm,sml->scjl", moved, sel_cols, precision=highest)
    re, im = moved[:, 0], moved[:, 1]
    pa = jnp.concatenate([re, re], -1).reshape(count * half, width)
    pb = jnp.concatenate([-im, im], -1).reshape(count * half, width)
    wl = jnp.broadcast_to(jnp.pad(source_weights, (0, 128 - count))[None], (8, 128))
    wb = jnp.broadcast_to(source_weights[:, None], (count, width))
    vmem = pl.BlockSpec(memory_space=pltpu.VMEM)
    src_sends = (ns - 1) * (2 + 2 * INNER_STEPS + 1)
    tile_sends = 2 + INNER_STEPS * (2 + nt - 1) + (nt - 1)
    args = (mask_param, target_image, wl, wb, pa, pb, *consts)
    mask_final, weights_final = pl.pallas_call(
        functools.partial(kernel, ns, nt, 1.0 / (period * size)),
        out_shape=(
            jax.ShapeDtypeStruct(mask_param.shape, f32),
            jax.ShapeDtypeStruct((8, 128), f32),
        ),
        in_specs=[vmem] * len(args),
        out_specs=(vmem, vmem),
        scratch_shapes=[
            pltpu.VMEM((period, size), f32),
            pltpu.VMEM((count, half, width), f32),
            pltpu.VMEM((2, MARGIN, size), f32),
            pltpu.VMEM((ns, 8, 128), f32),
            pltpu.VMEM((INNER_STEPS + 1, ns, half // 2, width), f32),
            pltpu.VMEM((INNER_STEPS, ns, half, width), f32),
            pltpu.VMEM((INNER_STEPS, 3, half, width), f32),
            pltpu.VMEM((INNER_STEPS, nt, 8, 128), f32),
            pltpu.VMEM((nt, 8, 128), f32),
            pltpu.VMEM((ns, 8, 128), f32),
            pltpu.SemaphoreType.DMA((src_sends,)),
            pltpu.SemaphoreType.DMA((src_sends,)),
            pltpu.SemaphoreType.DMA((tile_sends,)),
            pltpu.SemaphoreType.DMA((tile_sends,)),
        ],
        compiler_params=pltpu.CompilerParams(
            collective_id=0, has_side_effects=True, vmem_limit_bytes=48 * 1024 * 1024
        ),
    )(*args)
    return mask_final, weights_final[0, :count]


def solution(mesh):
    in_specs = (
        P(("group", "tile"), None),
        P(("group", "tile"), None),
        P(("group", "src")),
        P("src", None),
        P(),
    )
    out_specs = (P(("group", "tile"), None), P(("group", "src")))
    return jax.shard_map(
        functools.partial(per_device, mesh.shape["src"], mesh.shape["tile"]),
        mesh=mesh, in_specs=in_specs, out_specs=out_specs, check_vma=False,
    )
```

```python
import functools
import math

import jax
import jax.numpy as jnp
import numpy as np
from jax import lax
from jax.experimental import pallas as pl
from jax.experimental.pallas import tpu as pltpu
from jax.sharding import PartitionSpec as P

MARGIN = 64
MAX_SHIFT = 16
INNER_STEPS = 2
MESH = pl.DeviceIdType.MESH
mask_rate = 0.5
weight_rate = 0.3
tiny_eps = 1e-06
f32 = jnp.float32
bf16 = jnp.bfloat16


def angle(freqs, pixels, period):
    return np.mod(np.outer(freqs, pixels), period) * (2.0 * math.pi / period)


def dirichlet(pixels, period, box):
    grid = 2 * box
    diffs = np.arange(-(box - 1), box)
    left = angle(pixels, diffs, period)
    right = angle(diffs, np.arange(grid), grid)
    return (np.cos(left) @ np.cos(right) + np.sin(left) @ np.sin(right)) / grid


def tables(period, tile, box):
    grid = 2 * box
    wide = np.arange(grid) - box
    row = angle(wide, np.arange(period), period)
    col = angle(wide, np.arange(tile), period)
    g = angle(np.arange(grid), np.arange(grid), grid)
    c, s = np.cos(g), np.sin(g)
    k1 = dirichlet(np.arange(tile) + MARGIN, period, box)
    k2 = dirichlet(np.arange(tile), period, box)
    k2d = np.concatenate([k2.T, np.zeros_like(k2.T)], 0)
    return dict(
        rf=np.concatenate([np.cos(row), np.sin(row)], 0),
        cf=np.concatenate([np.cos(col), np.sin(col)], 0).T,
        c2=np.block([[c, s], [-s, c]]),
        c2t=np.block([[c, -s], [s, c]]),
        cs=np.concatenate([c, s], 0),
        k1=k1,
        k1t=k1.T,
        k2d=k2d,
        k2dt=np.concatenate([k2, k2], 1),
        col=np.block([[np.cos(col), np.sin(col)], [-np.sin(col), np.cos(col)]]),
        rfa=np.concatenate([np.cos(row), -np.sin(row)], 0).T,
    )


LEFT = ("rf", "cs", "k1", "k1t", "rfa")
NAMES = ("rf", "cf", "c2", "c2t", "cs", "k1", "k1t", "k2d", "k2dt", "col", "rfa")


def split_np(value):
    value = value.astype(np.float32)
    high = value.astype(jnp.bfloat16)
    low = (value - high.astype(np.float32)).astype(jnp.bfloat16)
    return high, low


def packed(name, value):
    high, low = split_np(value)
    if name in ("c2", "c2t"):
        return np.block([[high, low], [high, np.zeros_like(low)]])
    if name in LEFT:
        return np.concatenate([high, high, low], 1)
    return np.concatenate([high, high, low], 0)


def split(value):
    high = value.astype(bf16)
    return high, (value - high.astype(f32)).astype(bf16)


def dot(a, b):
    return jnp.dot(a, b, preferred_element_type=f32)


def left_dot(table, value):
    high, low = split(value)
    return dot(table, jnp.concatenate([high, low, high], 0))


def right_dot(value, table):
    high, low = split(value)
    return dot(jnp.concatenate([high, low, high], 1), table)


def wide_dot(value, table):
    high, low = split(value)
    both = dot(jnp.concatenate([high, low], 1), table)
    width = value.shape[1]
    return both[:, :width] + both[:, width:]


def kernel(ns, nt, scale, *refs):
    mask_ref, target_ref, wl_ref, wb_ref, pa_ref, pb_ref = refs[:6]
    consts = {name: refs[6 + i] for i, name in enumerate(NAMES)}
    refs = refs[6 + len(NAMES):]
    mask_out, weights_out = refs[:2]
    (params, grid, halo, dose_buf, power_buf, back_buf, next_buf, sq_buf, sg_buf,
     src_send, src_recv, tile_send, tile_recv, all_send, all_recv) = refs[2:]
    group = lax.axis_index("group")
    src = lax.axis_index("src")
    tile = lax.axis_index("tile")
    size = mask_ref.shape[1]
    period = size + 2 * MARGIN
    count = wb_ref.shape[0]
    width = pa_ref.shape[1]
    half = width // 2

    def table(name):
        return consts[name][...]

    def src_peer(r):
        return (group, lax.rem(src + r, ns), tile)

    def tile_peer(r):
        return (group, src, lax.rem(tile + r, nt))

    everyone = [(a, b) for a in range(ns) for b in range(nt) if a or b]

    def any_peer(a, b):
        return (group, lax.rem(src + a, ns), lax.rem(tile + b, nt))

    pending = []
    used = dict(src=0, tile=0, all=0)
    sems = dict(src=(src_send, src_recv), tile=(tile_send, tile_recv), all=(all_send, all_recv))

    def start(axis, source, target, peer):
        at = used[axis]
        used[axis] = at + 1
        sends, recvs = sems[axis]
        copy = pltpu.make_async_remote_copy(
            src_ref=source, dst_ref=target, send_sem=sends.at[at], recv_sem=recvs.at[at],
            device_id=peer, device_id_type=MESH,
        )
        copy.start()
        pending.append(copy)
        return copy

    def spread_src(buf):
        return [start("src", buf.at[src], buf.at[src], src_peer(r)) for r in range(1, ns)]

    def spread_tile(buf):
        return [start("tile", buf.at[tile], buf.at[tile], tile_peer(r)) for r in range(1, nt)]

    def landed(copies):
        for copy in copies:
            copy.wait_recv()

    def total(buf, peers):
        value = buf[0]
        for i in range(1, peers):
            value = value + buf[i]
        return value

    barrier = pltpu.get_barrier_semaphore()
    for a, b in everyone:
        pl.semaphore_signal(barrier, inc=1, device_id=any_peer(a, b), device_id_type=MESH)
    pl.semaphore_wait(barrier, ns * nt - 1)

    up = start("tile", mask_ref.at[pl.ds(size - MARGIN, MARGIN)], halo.at[0], tile_peer(1))
    down = start("tile", mask_ref.at[pl.ds(0, MARGIN)], halo.at[1], tile_peer(nt - 1))
    dose_buf[src] = wl_ref[...]
    dose_copies = spread_src(dose_buf)
    params[pl.ds(MARGIN, size)] = mask_ref[...]
    landed([up, down])
    params[pl.ds(0, MARGIN)] = halo[0]
    params[pl.ds(MARGIN + size, MARGIN)] = halo[1]

    has_prev = (tile > 0).astype(f32)
    has_next = (tile < nt - 1).astype(f32)
    row_id = lax.broadcasted_iota(jnp.int32, (period, size), 0)
    keep = jnp.where(row_id < MARGIN, has_prev, jnp.where(row_id >= MARGIN + size, has_next, 1.0))
    lane = lax.broadcasted_iota(jnp.int32, (half, width), 1)
    sign = jnp.where(lane < half, 1.0, -1.0).astype(f32)

    def swap(value):
        return pltpu.roll(value, half, 1)

    def sigmoid_mask():
        return keep / (1.0 + jnp.exp(-params[...]))

    def imaging(mask, step):
        quad = right_dot(left_dot(table("rf"), mask), table("cf")) * scale
        spec = sign * quad[:half] - swap(quad[half:])
        spec_swap = swap(spec)
        parts = []
        for s in range(count):
            rows = pl.ds(s * half, half)
            parts.append(pa_ref[rows] * spec + pb_ref[rows] * spec_swap)
        lit = jnp.concatenate(parts, 0)
        mid = wide_dot(lit, table("c2"))
        cs = table("cs")
        power = jnp.zeros((half, width), f32)
        for s in range(0, count, 2):
            pair = [mid[i * half:(i + 1) * half] for i in range(s, s + 2)]
            both = left_dot(cs, jnp.concatenate(pair, 1))
            for i in range(2):
                one = both[:, i * width:(i + 1) * width]
                z = one[:half] - sign * swap(one[half:])
                grid[s + i] = z
                power = power + wb_ref[s + i:s + i + 1] * (z * z)
        power = power + swap(power)
        power = jnp.where(lane[:half // 2] < half, power[:half // 2], power[half // 2:])
        buf = power_buf.at[step]
        buf[src] = power
        landed(spread_src(buf))
        power = total(buf, ns)
        if step == 0:
            landed(dose_copies)
        dose = jnp.sum(total(dose_buf, ns)[0:1], axis=1, keepdims=True)
        inv_dose = 1.0 / dose
        power = jnp.concatenate([power, swap(power)], 0)
        bright = right_dot(left_dot(table("k1"), power), table("k2d")) * inv_dose
        misfit = bright - target_ref[...]
        pull = right_dot(left_dot(table("k1t"), misfit), table("k2dt"))
        return bright, misfit, pull, inv_dose

    for step in range(INNER_STEPS):
        mask = sigmoid_mask()
        bright, misfit, pull, inv_dose = imaging(mask, step)
        cs = table("cs")
        parts = []
        for s in range(0, count, 2):
            pair = [pull * grid[i] for i in range(s, s + 2)]
            both = left_dot(cs, jnp.concatenate(pair, 1))
            for i in range(2):
                part = both[:, i * width:(i + 1) * width]
                parts.append(part[:half] + sign * swap(part[half:]))
        box = wide_dot(jnp.concatenate(parts, 0), table("c2t"))
        one = jnp.zeros((half, width), f32)
        two = jnp.zeros((half, width), f32)
        for s in range(count):
            rows = pl.ds(s * half, half)
            value = wb_ref[s:s + 1] * box[s * half:(s + 1) * half]
            one = one + pa_ref[rows] * value
            two = two + pb_ref[rows] * value
        buf = back_buf.at[step]
        buf[src] = (one + swap(two)) * (2.0 * scale * inv_dose)
        landed(spread_src(buf))
        own = next_buf.at[step]
        back = total(buf, ns)
        own[2] = back
        to_next = start("tile", own.at[2], own.at[0], tile_peer(1))
        to_prev = start("tile", own.at[2], own.at[1], tile_peer(nt - 1))
        col = table("col")

        def values(spectrum):
            wide = right_dot(spectrum, col)
            return jnp.concatenate([wide[:, :size], wide[:, size:]], 0)

        grad = left_dot(table("rfa"), values(back))
        landed([to_next, to_prev])
        rim = 2 * MARGIN
        rfa = consts["rfa"]
        before = left_dot(rfa[pl.ds(period - rim, rim)], values(own[0] * has_prev))
        after = left_dot(rfa[pl.ds(0, rim)], values(own[1] * has_next))
        grad = jnp.concatenate(
            [grad[:rim] + before, grad[rim:period - rim], grad[period - rim:] + after], 0
        )
        grad = grad * (mask * (1.0 - mask))
        core = grad[MARGIN:MARGIN + size]
        square = jnp.sum(core * core, axis=0, keepdims=True)
        square = jnp.sum(square, axis=1, keepdims=True)
        buf = sq_buf.at[step]
        buf[tile] = jnp.broadcast_to(square, sq_buf.shape[2:])
        landed(spread_tile(buf))
        square = total(buf, nt)[0:1, 0:1]
        rms = jnp.sqrt(square / float(nt * size * size) + tiny_eps)
        params[...] = params[...] - grad * (mask_rate / rms)
    mask_out[...] = params[pl.ds(MARGIN, size)]

    bright, misfit, pull, inv_dose = imaging(sigmoid_mask(), INNER_STEPS)
    level = jnp.sum(misfit * bright, axis=0, keepdims=True)
    level = jnp.sum(level, axis=1, keepdims=True)
    rows = []
    for s in range(count):
        rows.append(jnp.sum(pull * (grid[s] * grid[s]), axis=0, keepdims=True))
    sums = jnp.sum(jnp.concatenate(rows, 0), axis=1, keepdims=True)
    sums = (sums - level) * inv_dose
    lanes = lax.broadcasted_iota(jnp.int32, (count, 128), 1)
    ids = lax.broadcasted_iota(jnp.int32, (count, 128), 0)
    ordered = jnp.sum(jnp.where(lanes == ids, sums, 0.0), axis=0, keepdims=True)
    here = src * nt + tile
    sg_buf[here] = jnp.broadcast_to(ordered, (8, 128))
    landed([start("all", sg_buf.at[here], sg_buf.at[here], any_peer(a, b)) for a, b in everyone])
    square = jnp.zeros((8, 128), f32)
    for k in range(ns):
        one = sg_buf[k * nt]
        for i in range(1, nt):
            one = one + sg_buf[k * nt + i]
        square = square + one * one
    slope = sg_buf[src * nt]
    for i in range(1, nt):
        slope = slope + sg_buf[src * nt + i]
    square = jnp.sum(square[0:1], axis=1, keepdims=True)
    spread = jnp.sqrt(square / float(count * ns) + tiny_eps)
    weights_out[...] = wl_ref[...] * jnp.exp(-weight_rate * slope / spread)
    for copy in pending:
        copy.wait_send()


def per_device(ns, nt, mask_param, target_image, source_weights, source_shifts, pupil_map):
    size = mask_param.shape[1]
    box = pupil_map.shape[1]
    half = 2 * box
    width = 2 * half
    count = source_weights.shape[0]
    period = size + 2 * MARGIN
    consts = []
    made = tables(period, size, box)
    for name in NAMES:
        consts.append(jnp.asarray(packed(name, made[name])))
    highest = lax.Precision.HIGHEST
    base = jnp.arange(box, dtype=jnp.int32)[None, :, None] + MAX_SHIFT
    columns = jnp.arange(half, dtype=jnp.int32)[None, None, :]
    sel_rows = (base + source_shifts[:, 0, None, None] == columns).astype(f32)
    sel_cols = (base + source_shifts[:, 1, None, None] == columns).astype(f32)
    moved = jnp.einsum("cim,sij->scjm", pupil_map, sel_rows, precision=highest)
    moved = jnp.einsum("scjm,sml->scjl", moved, sel_cols, precision=highest)
    re, im = moved[:, 0], moved[:, 1]
    pa = jnp.concatenate([re, re], -1).reshape(count * half, width)
    pb = jnp.concatenate([-im, im], -1).reshape(count * half, width)
    wl = jnp.broadcast_to(jnp.pad(source_weights, (0, 128 - count))[None], (8, 128))
    wb = jnp.broadcast_to(source_weights[:, None], (count, width))
    vmem = pl.BlockSpec(memory_space=pltpu.VMEM)
    src_sends = (ns - 1) * (2 + 2 * INNER_STEPS)
    tile_sends = 2 + INNER_STEPS * (2 + nt - 1)
    args = (mask_param, target_image, wl, wb, pa, pb, *consts)
    mask_final, weights_final = pl.pallas_call(
        functools.partial(kernel, ns, nt, 1.0 / (period * size)),
        out_shape=(
            jax.ShapeDtypeStruct(mask_param.shape, f32),
            jax.ShapeDtypeStruct((8, 128), f32),
        ),
        in_specs=[vmem] * len(args),
        out_specs=(vmem, vmem),
        scratch_shapes=[
            pltpu.VMEM((period, size), f32),
            pltpu.VMEM((count, half, width), f32),
            pltpu.VMEM((2, MARGIN, size), f32),
            pltpu.VMEM((ns, 8, 128), f32),
            pltpu.VMEM((INNER_STEPS + 1, ns, half // 2, width), f32),
            pltpu.VMEM((INNER_STEPS, ns, half, width), f32),
            pltpu.VMEM((INNER_STEPS, 3, half, width), f32),
            pltpu.VMEM((INNER_STEPS, nt, 8, 128), f32),
            pltpu.VMEM((ns * nt, 8, 128), f32),
            pltpu.SemaphoreType.DMA((src_sends,)),
            pltpu.SemaphoreType.DMA((src_sends,)),
            pltpu.SemaphoreType.DMA((tile_sends,)),
            pltpu.SemaphoreType.DMA((tile_sends,)),
            pltpu.SemaphoreType.DMA((ns * nt - 1,)),
            pltpu.SemaphoreType.DMA((ns * nt - 1,)),
        ],
        compiler_params=pltpu.CompilerParams(
            collective_id=0, has_side_effects=True, vmem_limit_bytes=48 * 1024 * 1024
        ),
    )(*args)
    return mask_final, weights_final[0, :count]


def solution(mesh):
    in_specs = (
        P(("group", "tile"), None),
        P(("group", "tile"), None),
        P(("group", "src")),
        P("src", None),
        P(),
    )
    out_specs = (P(("group", "tile"), None), P(("group", "src")))
    return jax.shard_map(
        functools.partial(per_device, mesh.shape["src"], mesh.shape["tile"]),
        mesh=mesh, in_specs=in_specs, out_specs=out_specs, check_vma=False,
    )
```
